32 devices in a mesh: dp: 8 (over z, x), tensor: 4 (over y, core).
Axes of the slice: x: 2, y: 2, z: 4, core: 2. Of those that a mesh axis runs over, the one named last changes fastest.
Arguments:
- tokens: bfloat16 [2, 8192, 1024], P(None, ('dp', 'tensor')), may hold values from -6 to 6
- condition: bfloat16 [2, 8, 1024], P(None, 'dp'), may hold values from -6 to 6
- cotangent: bfloat16 [2, 8192, 1024], P(None, ('dp', 'tensor')), may hold values from -6 to 6
- adaptive_weight: bfloat16 [6, 1024, 1024], P(None, 'dp', 'tensor'), may hold values from -0.1875 to 0.1875
- adaptive_bias: bfloat16 [6, 1024], P(None, ('tensor', 'dp')), may hold values from -1.796875 to 1.796875
- inward_weight: bfloat16 [1024, 16, 192], P('dp', 'tensor'), may hold values from -0.1875 to 0.1875
- inward_bias: bfloat16 [16, 128], P('tensor', 'dp'), may hold values from -1.796875 to 1.796875
- outward_weight: bfloat16 [16, 64, 1024], P('tensor', None, 'dp'), may hold values from -0.8984375 to 0.8984375
- outward_bias: bfloat16 [1024], P(('tensor', 'dp')), may hold values from -1.796875 to 1.796875
- expand_weight: bfloat16 [1024, 4096], P('dp', 'tensor'), may hold values from -0.1875 to 0.1875
- expand_bias: bfloat16 [4096], P(('tensor', 'dp')), may hold values from -1.796875 to 1.796875
- shrink_weight: bfloat16 [4096, 1024], P('tensor', 'dp'), may hold values from -0.09375 to 0.09375
- shrink_bias: bfloat16 [1024], P(('tensor', 'dp')), may hold values from -1.796875 to 1.796875
Outputs:
- result: bfloat16 [2, 8192, 1024], P(None, ('dp', 'tensor'))
- tokens_grad: float32 [2, 8192, 1024], P(None, ('dp', 'tensor'))
- condition_grad: float32 [2, 8, 1024], P(None, 'dp')
- adaptive_weight_grad: float32 [6, 1024, 1024], P(None, 'dp', 'tensor')
- adaptive_bias_grad: float32 [6, 1024], P(None, ('tensor', 'dp'))
- inward_weight_grad: float32 [1024, 16, 192], P('dp', 'tensor')
- inward_bias_grad: float32 [16, 128], P('tensor', 'dp')
- outward_weight_grad: float32 [16, 64, 1024], P('tensor', None, 'dp')
- outward_bias_grad: float32 [1024], P(('tensor', 'dp'))
- expand_weight_grad: float32 [1024, 4096], P('dp', 'tensor')
- expand_bias_grad: float32 [4096], P(('tensor', 'dp'))
- shrink_weight_grad: float32 [4096, 1024], P('tensor', 'dp')
- shrink_bias_grad: float32 [1024], P(('tensor', 'dp'))
The draws below stay inside these ranges and needn't reach their ends.
All inputs are finite; a program needn't handle non-finite values.
Results may differ from the reference program's by a relative error of at most 0.02.
Values may be sent and summed in bfloat16 or wider, within the bound.
A program may use at most 256 MiB of HBM per device.

```python
import jax
import jax.numpy as jnp
from jax import lax

D = 1024
HEADS = 16
HD = 64
FF = 4096
SEQ = 1024
MB = 2
LATENTS = 8
TOKENS = 8192


def block_levels(rng, shape, cuts, low, largest):
    factor_of = 1.0
    for axis_at, shards_of in cuts:
        steps = jax.random.uniform(jax.random.fold_in(jax.random.fold_in(rng, 6), axis_at), (shards_of,), jnp.float32, low / len(cuts), largest / len(cuts))
        factor_of = factor_of * jnp.repeat(jnp.exp(steps), shape[axis_at] // shards_of).reshape((-1,) + (1,) * (len(shape) - 1 - axis_at))
    return factor_of


def normal_values(stream_key, dims, spread, reach, shards=(), held_as=jnp.bfloat16):
    array = jax.random.normal(stream_key, dims, jnp.float32) * spread
    if len(shards) > 0:
        array = block_levels(stream_key, dims, shards, -0.22, 0.18) * array
    return jnp.clip(array, min=-reach, max=reach).astype(held_as)


def setup_inputs(seed: int = 0) -> dict:
    key_of = jax.random.split(jax.random.key(seed), 14)
    return {
        "tokens": normal_values(key_of[0], (MB, TOKENS, D), 1.0, 6.0, ((1, 32),)),
        "condition": normal_values(key_of[1], (MB, LATENTS, D), 1.0, 6.0, ((1, 8),)),
        "cotangent": normal_values(key_of[2], (MB, TOKENS, D), 1.0, 6.0, ((1, 32),)),
        "adaptive_weight": normal_values(key_of[3], (6, D, D), D ** -0.5, 0.1875, ((1, 8), (2, 4))),
        "adaptive_bias": normal_values(key_of[4], (6, D), 0.3, 1.796875, ((1, 32),)),
        "inward_weight": normal_values(key_of[5], (D, HEADS, 3 * HD), D ** -0.5, 0.1875, ((0, 8), (1, 4))),
        "inward_bias": normal_values(key_of[6], (HEADS, 2 * HD), 0.3, 1.796875, ((0, 4), (1, 8))),
        "outward_weight": normal_values(key_of[7], (HEADS, HD, D), 0.15, 0.8984375, ((0, 4), (2, 8))),
        "outward_bias": normal_values(key_of[8], (D,), 0.3, 1.796875, ((0, 32),)),
        "expand_weight": normal_values(key_of[9], (D, FF), D ** -0.5, 0.1875, ((0, 8), (1, 4))),
        "expand_bias": normal_values(key_of[10], (FF,), 0.3, 1.796875, ((0, 32),)),
        "shrink_weight": normal_values(key_of[11], (FF, D), FF ** -0.5, 0.09375, ((0, 4), (1, 8))),
        "shrink_bias": normal_values(key_of[12], (D,), 0.3, 1.796875, ((0, 32),)),
    }


@jax.custom_vjp
def low(v):
    return lax.optimization_barrier(v.astype(jnp.bfloat16)).astype(jnp.float32)

@jax.custom_vjp
def low_back(v):
    return v

def low_keep(v):
    return (low(v), None)

def low_pass(kept, grad):
    return (grad,)

def back_keep(v):
    return (v, None)

def back_low(kept, grad):
    return (low(grad),)
low.defvjp(low_keep, low_pass)
low_back.defvjp(back_keep, back_low)
epsilon = 1e-06

def normalize(value):
    centered = value - lax.optimization_barrier(jnp.mean(value, axis=-1, keepdims=True))
    spread_sq = lax.optimization_barrier(jnp.mean(centered * centered, axis=-1, keepdims=True))
    return centered * lax.rsqrt(spread_sq + epsilon)

def layer_one(tokens, condition, adaptive_weight, adaptive_bias, inward_weight, inward_bias, outward_weight, outward_bias, expand_weight, expand_bias, shrink_weight, shrink_bias):
    highest = lax.Precision.HIGHEST
    cond_act = low(jax.nn.silu(condition))
    modulation = low_back(jnp.einsum('i,kio->ko', cond_act, adaptive_weight, precision=highest) + adaptive_bias)
    shift_one = modulation[0]
    scale_one = modulation[1]
    gate_one = modulation[2]
    shift_two = modulation[3]
    scale_two = modulation[4]
    gate_two = modulation[5]
    mixed_in = low(normalize(tokens) * (1.0 + scale_one) + shift_one)
    zeros_mid = jnp.zeros((HEADS, HD), jnp.float32)
    bias_full = jnp.concatenate([inward_bias[:, :HD], zeros_mid, inward_bias[:, HD:]], axis=1)
    packed = jnp.einsum('si,iht->sht', mixed_in, inward_weight, precision=highest) + bias_full
    packed = low(low_back(packed))
    query = packed[..., :HD]
    keys = packed[..., HD:2 * HD]
    values = packed[..., 2 * HD:]
    scores = low_back(jnp.einsum('qhd,khd->hqk', query, keys, precision=highest) * HD ** (-0.5))
    weights = jax.nn.softmax(scores, axis=-1)
    attended = jnp.einsum('hqk,khd->qhd', low(weights), values, precision=highest)
    attended = low(low_back(attended))
    attn_out = low_back(jnp.einsum('shd,hdo->so', attended, outward_weight, precision=highest) + outward_bias)
    first_sum = tokens + gate_one * attn_out
    mlp_in = low(normalize(first_sum) * (1.0 + scale_two) + shift_two)
    hidden = low_back(jnp.dot(mlp_in, expand_weight, precision=highest) + expand_bias)
    active = low(jax.nn.gelu(hidden, approximate=True))
    mlp_out = low_back(jnp.dot(active, shrink_weight, precision=highest) + shrink_bias)
    return first_sum + gate_two * mlp_out

def reference(tokens, condition, cotangent, adaptive_weight, adaptive_bias, inward_weight, inward_bias, outward_weight, outward_bias, expand_weight, expand_bias, shrink_weight, shrink_bias):
    count = MB * LATENTS
    inputs = tokens.astype(jnp.float32).reshape(count, SEQ, D)
    conds = condition.astype(jnp.float32).reshape(count, D)
    seeds = cotangent.astype(jnp.float32).reshape(count, SEQ, D)
    params = tuple((weight.astype(jnp.float32) for weight in (adaptive_weight, adaptive_bias, inward_weight, inward_bias, outward_weight, outward_bias, expand_weight, expand_bias, shrink_weight, shrink_bias)))

    def advance(totals, item):
        tokens_one, condition_one, seed_one = item
        result_one, pull = jax.vjp(layer_one, tokens_one, condition_one, *params)
        grads = pull(seed_one)
        totals = tuple((total + grad for total, grad in zip(totals, grads[2:])))
        return (totals, (result_one, grads[0], grads[1]))
    zeros_all = tuple((jnp.zeros_like(weight) for weight in params))
    totals, (results, token_grads, cond_grads) = lax.scan(advance, zeros_all, (inputs, conds, seeds))
    return (results.reshape(MB, TOKENS, D).astype(jnp.bfloat16), token_grads.reshape(MB, TOKENS, D), cond_grads.reshape(MB, LATENTS, D), totals[0], totals[1], totals[2], totals[3], totals[4], totals[5], totals[6], totals[7], totals[8], totals[9])
```

```python
import jax
import jax.numpy as jnp
from jax import lax
from jax.sharding import PartitionSpec as P

epsilon = 1e-06


def normalize(value):
    centered = value - jnp.mean(value, axis=-1, keepdims=True)
    inverse = lax.rsqrt(jnp.mean(centered * centered, axis=-1, keepdims=True) + epsilon)
    return (centered * inverse, inverse)


def normalize_back(normed, inverse, grad_normed):
    first = jnp.mean(grad_normed, axis=-1, keepdims=True)
    second = jnp.mean(grad_normed * normed, axis=-1, keepdims=True)
    return inverse * (grad_normed - first - normed * second)


def gather_rows(value):
    size = lax.axis_size("tensor")
    me = lax.axis_index("tensor")
    parts = value[None]
    bit = size // 2
    while bit >= 1:
        other = lax.ppermute(parts, "tensor", [(one, one ^ bit) for one in range(size)])
        low = lax.rem(me // bit, 2) == 0
        parts = jnp.stack(
            [jnp.where(low, parts, other), jnp.where(low, other, parts)], axis=1
        ).reshape(2 * parts.shape[0], *value.shape)
        bit //= 2
    return parts.reshape(size * value.shape[0], *value.shape[1:])


def sum_rows(value):
    size = lax.axis_size("tensor")
    me = lax.axis_index("tensor")
    parts = value.reshape(size, value.shape[0] // size, *value.shape[1:])
    bit = 1
    while bit < size:
        pairs = parts.reshape(parts.shape[0] // 2, 2, *parts.shape[1:])
        low = lax.rem(me // bit, 2) == 0
        keep = jnp.where(low, pairs[:, 0], pairs[:, 1])
        send = jnp.where(low, pairs[:, 1], pairs[:, 0]).astype(jnp.bfloat16)
        other = lax.ppermute(send, "tensor", [(one, one ^ bit) for one in range(size)])
        parts = keep + other.astype(jnp.float32)
        bit *= 2
    return parts[0]


def shifted(size, step):
    return [(source, (source + step) % size) for source in range(size)]


def exchange_dp(pick):
    size = lax.axis_size("dp")
    me = lax.axis_index("dp")
    return [pick(me)] + [
        lax.ppermute(pick(lax.rem(me + step, size)), "dp", shifted(size, step))
        for step in range(1, size)
    ]


def by_source(parts):
    size = lax.axis_size("dp")
    me = lax.axis_index("dp")
    order = lax.rem(me + size - jnp.arange(size, dtype=jnp.int32), size)
    return jnp.take(jnp.stack(parts), order, axis=0, mode="clip")


def at(value, index):
    return lax.dynamic_index_in_dim(value, index, 0, keepdims=False)


def attend_forward(query, keys, values, block, scale):
    outputs = []
    totals = []
    for begin in range(0, query.shape[0], block):
        rows = query[begin : begin + block]
        scores = jnp.einsum("qhd,khd->hqk", rows, keys, preferred_element_type=jnp.float32) * scale
        peak = jnp.max(scores, axis=-1, keepdims=True)
        raised = jnp.exp(scores - peak)
        total = jnp.sum(raised, axis=-1, keepdims=True)
        weights = (raised / total).astype(jnp.bfloat16)
        outputs.append(
            jnp.einsum("hqk,khd->qhd", weights, values, preferred_element_type=jnp.float32)
        )
        totals.append(peak + jnp.log(total))
    return (jnp.concatenate(outputs, axis=0), jnp.concatenate(totals, axis=1))


def attend_backward(query, keys, values, logsum, grad_out, block, scale):
    grad_keys = jnp.zeros(keys.shape, jnp.float32)
    grad_values = jnp.zeros(values.shape, jnp.float32)
    grad_parts = []
    for begin in range(0, query.shape[0], block):
        rows = query[begin : begin + block]
        grad_rows = grad_out[begin : begin + block]
        scores = jnp.einsum("qhd,khd->hqk", rows, keys, preferred_element_type=jnp.float32) * scale
        weights = jnp.exp(scores - logsum[:, begin : begin + block])
        grad_weights = jnp.einsum(
            "qhd,khd->hqk", grad_rows, values, preferred_element_type=jnp.float32
        )
        inner = jnp.sum(grad_weights * weights, axis=-1, keepdims=True)
        grad_scores = (weights * (grad_weights - inner)).astype(jnp.bfloat16)
        grad_parts.append(
            jnp.einsum("hqk,khd->qhd", grad_scores, keys, preferred_element_type=jnp.float32)
            * scale
        )
        grad_keys = (
            grad_keys
            + jnp.einsum("hqk,qhd->khd", grad_scores, rows, preferred_element_type=jnp.float32)
            * scale
        )
        grad_values = grad_values + jnp.einsum(
            "hqk,qhd->khd",
            weights.astype(jnp.bfloat16),
            grad_rows,
            preferred_element_type=jnp.float32,
        )
    return (jnp.concatenate(grad_parts, axis=0), grad_keys, grad_values)


def body(
    tokens,
    condition,
    cotangent,
    adaptive_weight,
    adaptive_bias,
    inward_weight,
    inward_bias,
    outward_weight,
    outward_bias,
    expand_weight,
    expand_bias,
    shrink_weight,
    shrink_bias,
):
    tensor_size = lax.axis_size("tensor")
    micro, tok_rows, width = tokens.shape
    latents = condition.shape[1]
    group_rows = tok_rows * tensor_size
    seq_len = group_rows // latents
    heads_local = outward_weight.shape[0]
    head_size = outward_weight.shape[1]
    hidden_local = shrink_weight.shape[0]
    block = min(512, seq_len)
    scale = head_size ** (-0.5)

    def attn_params():
        return (
            lax.all_gather(inward_weight, "dp", axis=0, tiled=True),
            lax.all_gather(inward_bias, "dp", axis=1, tiled=True),
            lax.all_gather(outward_weight, "dp", axis=2, tiled=True),
        )

    def mlp_params():
        pieces = (
            lax.all_gather(expand_weight, "dp", axis=0, tiled=True),
            lax.all_gather(expand_bias, "dp", axis=0, tiled=True),
            lax.all_gather(shrink_weight, "dp", axis=1, tiled=True),
        )
        return pieces

    dp_size = lax.axis_size("dp")
    dp_at = lax.axis_index("dp")
    pairs = micro * latents
    rows_piece = adaptive_weight.shape[1]
    cols_piece = adaptive_weight.shape[2]
    cond_float = condition.astype(jnp.float32)
    cond_act = jax.nn.silu(cond_float).astype(jnp.bfloat16)
    packet = jnp.concatenate(
        [
            jnp.pad(part.reshape(-1, outward_bias.shape[0]), ((0, 0), (0, 128 - outward_bias.shape[0])))
            for part in (adaptive_bias, outward_bias, shrink_bias)
        ]
    )
    spread = by_source(exchange_dp(lambda target: packet))[:, :, : outward_bias.shape[0]]
    ada_bias = spread[:, :6].transpose(1, 0, 2).reshape(6, cols_piece)
    outward_piece = spread[:, 6].reshape(-1)
    shrink_piece = spread[:, 7].reshape(-1)
    cond_all = by_source(exchange_dp(lambda target: cond_act.reshape(pairs, width)))
    cond_mine = lax.dynamic_slice_in_dim(
        cond_all.reshape(dp_size * pairs, width), dp_at * rows_piece, rows_piece, 1
    )
    partial = jnp.einsum(
        "bi,kio->bko", cond_mine, adaptive_weight, preferred_element_type=jnp.float32
    ).reshape(dp_size, pairs, 6, cols_piece)
    mod_part = sum(exchange_dp(lambda target: at(partial, target)))
    mod_part = mod_part.reshape(micro, latents, 6, cols_piece) + ada_bias.astype(jnp.float32)
    modulation, proj_bias, out_bias = (
        lax.all_gather(mod_part, "tensor", axis=3, tiled=True),
        lax.all_gather(outward_piece.astype(jnp.float32), "tensor", axis=0, tiled=True),
        lax.all_gather(shrink_piece.astype(jnp.float32), "tensor", axis=0, tiled=True),
    )
    first_row = lax.axis_index("tensor") * tok_rows
    owner = (first_row + jnp.arange(tok_rows, dtype=jnp.int32)) // seq_len
    member = (owner[:, None] == jnp.arange(latents, dtype=jnp.int32)[None, :]).astype(jnp.float32)
    states = []
    outputs = []
    for index in range(micro):
        rows_mod = jnp.dot(
            member, modulation[index].reshape(latents, 6 * width), precision=lax.Precision.HIGHEST
        ).reshape(tok_rows, 6, width)
        inputs = tokens[index].astype(jnp.float32)
        normed_one, inverse_one = normalize(inputs)
        mixed_in = (normed_one * (1.0 + rows_mod[:, 1]) + rows_mod[:, 0]).astype(jnp.bfloat16)
        attn_weight, qv_bias, proj_weight = attn_params()
        mixed_full = gather_rows(mixed_in)
        qkv_bias = jnp.concatenate(
            [
                qv_bias[:, :head_size],
                jnp.zeros((heads_local, head_size), jnp.bfloat16),
                qv_bias[:, head_size:],
            ],
            axis=1,
        ).astype(jnp.float32)
        projected = jnp.dot(
            mixed_full,
            attn_weight.reshape(width, heads_local * 3 * head_size),
            preferred_element_type=jnp.float32,
        )
        packed = (projected.reshape(group_rows, heads_local, 3 * head_size) + qkv_bias).astype(
            jnp.bfloat16
        )
        packed_seq = packed.reshape(latents, seq_len, heads_local, 3 * head_size)
        query = packed_seq[..., :head_size]
        keys = packed_seq[..., head_size : 2 * head_size]
        values = packed_seq[..., 2 * head_size :]
        attended, logsum = lax.map(
            lambda item: attend_forward(item[0], item[1], item[2], block, scale),
            (query, keys, values),
        )
        attended = attended.astype(jnp.bfloat16).reshape(group_rows, heads_local * head_size)
        attn_terms = jnp.dot(
            attended,
            proj_weight.reshape(heads_local * head_size, width),
            preferred_element_type=jnp.float32,
        )
        attn_out = sum_rows(attn_terms) + proj_bias
        first_sum = inputs + rows_mod[:, 2] * attn_out
        normed_two, inverse_two = normalize(first_sum)
        mlp_in = (normed_two * (1.0 + rows_mod[:, 4]) + rows_mod[:, 3]).astype(jnp.bfloat16)
        fc_in, fc_bias, fc_out = mlp_params()
        state = {}
        mlp_full = gather_rows(mlp_in)
        hidden = jnp.dot(mlp_full, fc_in, preferred_element_type=jnp.float32) + fc_bias.astype(
            jnp.float32
        )
        active = jax.nn.gelu(hidden, approximate=True).astype(jnp.bfloat16)
        mlp_out = sum_rows(jnp.dot(active, fc_out, preferred_element_type=jnp.float32)) + out_bias
        outputs.append((first_sum + rows_mod[:, 5] * mlp_out).astype(jnp.bfloat16))
        state.update(
            {
                "rows_mod": rows_mod,
                "normed_one": normed_one,
                "inverse_one": inverse_one,
                "mixed_in": mixed_in,
                "query": query,
                "keys": keys,
                "values": values,
                "logsum": logsum,
                "attended": attended,
                "attn_out": attn_out,
                "normed_two": normed_two,
                "inverse_two": inverse_two,
                "mlp_in": mlp_in,
                "hidden": hidden,
                "active": active,
                "mlp_out": mlp_out,
            }
        )
        states.append(state)
    acc_qkv = jnp.zeros((width, heads_local, 3 * head_size), jnp.float32)
    acc_qv = jnp.zeros((heads_local, 2 * head_size), jnp.float32)
    acc_proj = jnp.zeros((heads_local, head_size, width), jnp.float32)
    acc_proj_bias = jnp.zeros((width,), jnp.float32)
    acc_fc_in = jnp.zeros((width, hidden_local), jnp.float32)
    acc_fc_bias = jnp.zeros((hidden_local,), jnp.float32)
    acc_fc_out = jnp.zeros((hidden_local, width), jnp.float32)
    acc_out_bias = jnp.zeros((width,), jnp.float32)
    mod_grads = []
    token_grads = []
    for index in range(micro):
        state = states[index]
        rows_mod = state["rows_mod"]
        attn_weight, qv_bias, proj_weight = attn_params()
        fc_in, fc_bias, fc_out = mlp_params()
        mixed_full = gather_rows(state["mixed_in"])
        grad_two = cotangent[index].astype(jnp.float32)
        grad_mlp = (rows_mod[:, 5] * grad_two).astype(jnp.bfloat16)
        acc_out_bias = acc_out_bias + jnp.sum(grad_mlp, axis=0, dtype=jnp.float32)
        unused, pull = jax.vjp(lambda value: jax.nn.gelu(value, approximate=True), state["hidden"])
        mlp_full = gather_rows(state["mlp_in"])
        grad_mlp_full = gather_rows(grad_mlp)
        acc_fc_out = acc_fc_out + jnp.einsum(
            "th,to->ho", state["active"], grad_mlp_full, preferred_element_type=jnp.float32
        )
        grad_active = jnp.einsum(
            "to,ho->th", grad_mlp_full, fc_out, preferred_element_type=jnp.float32
        )
        grad_hidden = pull(grad_active)[0].astype(jnp.bfloat16)
        acc_fc_bias = acc_fc_bias + jnp.sum(grad_hidden, axis=0, dtype=jnp.float32)
        acc_fc_in = acc_fc_in + jnp.einsum(
            "ti,th->ih", mlp_full, grad_hidden, preferred_element_type=jnp.float32
        )
        grad_mlp_in = sum_rows(
            jnp.einsum("th,ih->ti", grad_hidden, fc_in, preferred_element_type=jnp.float32)
        )
        normed_two = state["normed_two"]
        grad_first = grad_two + normalize_back(
            normed_two, state["inverse_two"], grad_mlp_in * (1.0 + rows_mod[:, 4])
        )
        grad_attn = (rows_mod[:, 2] * grad_first).astype(jnp.bfloat16)
        acc_proj_bias = acc_proj_bias + jnp.sum(grad_attn, axis=0, dtype=jnp.float32)
        grad_attn_full = gather_rows(grad_attn)
        acc_proj = acc_proj + jnp.einsum(
            "tc,to->co", state["attended"], grad_attn_full, preferred_element_type=jnp.float32
        ).reshape(heads_local, head_size, width)
        grad_attended = jnp.einsum(
            "to,co->tc",
            grad_attn_full,
            proj_weight.reshape(heads_local * head_size, width),
            preferred_element_type=jnp.float32,
        ).astype(jnp.bfloat16)
        grad_attended = grad_attended.reshape(latents, seq_len, heads_local, head_size)
        grad_query, grad_keys, grad_values = lax.map(
            lambda item: attend_backward(item[0], item[1], item[2], item[3], item[4], block, scale),
            (state["query"], state["keys"], state["values"], state["logsum"], grad_attended),
        )
        grad_packed = jnp.concatenate([grad_query, grad_keys, grad_values], axis=-1).astype(
            jnp.bfloat16
        )
        grad_packed = grad_packed.reshape(group_rows, heads_local, 3 * head_size)
        summed = jnp.sum(grad_packed, axis=0, dtype=jnp.float32)
        acc_qv = acc_qv + jnp.concatenate(
            [summed[:, :head_size], summed[:, 2 * head_size :]], axis=1
        )
        acc_qkv = acc_qkv + jnp.einsum(
            "ti,thc->ihc", mixed_full, grad_packed, preferred_element_type=jnp.float32
        )
        grad_mixed = sum_rows(
            jnp.einsum("thc,ihc->ti", grad_packed, attn_weight, preferred_element_type=jnp.float32)
        )
        normed_one = state["normed_one"]
        token_grads.append(
            grad_first
            + normalize_back(normed_one, state["inverse_one"], grad_mixed * (1.0 + rows_mod[:, 1]))
        )
        rows_grad = jnp.stack(
            [
                grad_mixed,
                grad_mixed * normed_one,
                grad_first * state["attn_out"],
                grad_mlp_in,
                grad_mlp_in * normed_two,
                grad_two * state["mlp_out"],
            ],
            axis=1,
        )
        mod_grads.append(
            jnp.einsum(
                "tl,tc->lc",
                member,
                rows_grad.reshape(tok_rows, 6 * width),
                precision=lax.Precision.HIGHEST,
            ).reshape(latents, 6, width)
        )
    mod_share, proj_bias_share, out_bias_share = (
        lax.psum_scatter(
            jnp.stack(mod_grads).astype(jnp.bfloat16), "tensor", scatter_dimension=3, tiled=True
        ).astype(jnp.float32),
        lax.psum_scatter(
            acc_proj_bias.astype(jnp.bfloat16), "tensor", scatter_dimension=0, tiled=True
        ).astype(jnp.float32),
        lax.psum_scatter(
            acc_out_bias.astype(jnp.bfloat16), "tensor", scatter_dimension=0, tiled=True
        ).astype(jnp.float32),
    )
    mod_low = mod_share.astype(jnp.bfloat16)
    mod_all = by_source(
        exchange_dp(lambda target: mod_low.reshape(pairs, 6, cols_piece))
    ).reshape(dp_size * pairs, 6, cols_piece)
    grad_ada = jnp.einsum("bi,bko->kio", cond_mine, mod_all, preferred_element_type=jnp.float32)
    grad_ada_bias = lax.dynamic_slice_in_dim(
        jnp.sum(mod_all, axis=0, dtype=jnp.float32),
        dp_at * adaptive_bias.shape[1],
        adaptive_bias.shape[1],
        1,
    )
    cond_back = jnp.einsum(
        "bko,kio->bi", mod_all, adaptive_weight, preferred_element_type=jnp.float32
    ).reshape(dp_size, pairs, rows_piece)
    cond_mix = by_source(exchange_dp(lambda target: at(cond_back, target)))
    cond_total = lax.psum(
        cond_mix.transpose(1, 0, 2).reshape(condition.shape).astype(jnp.bfloat16), "tensor"
    ).astype(jnp.float32)
    unused, pull_cond = jax.vjp(jax.nn.silu, cond_float)
    grad_cond = pull_cond(cond_total)[0]
    shares = (
        grad_ada,
        grad_ada_bias,
        lax.psum_scatter(
            acc_qkv.astype(jnp.bfloat16), "dp", scatter_dimension=0, tiled=True
        ).astype(jnp.float32),
        lax.psum_scatter(acc_qv.astype(jnp.bfloat16), "dp", scatter_dimension=1, tiled=True).astype(
            jnp.float32
        ),
        lax.psum_scatter(
            acc_proj.astype(jnp.bfloat16), "dp", scatter_dimension=2, tiled=True
        ).astype(jnp.float32),
        lax.psum_scatter(
            proj_bias_share.astype(jnp.bfloat16), "dp", scatter_dimension=0, tiled=True
        ).astype(jnp.float32),
        lax.psum_scatter(
            acc_fc_in.astype(jnp.bfloat16), "dp", scatter_dimension=0, tiled=True
        ).astype(jnp.float32),
        lax.psum_scatter(
            acc_fc_bias.astype(jnp.bfloat16), "dp", scatter_dimension=0, tiled=True
        ).astype(jnp.float32),
        lax.psum_scatter(
            acc_fc_out.astype(jnp.bfloat16), "dp", scatter_dimension=1, tiled=True
        ).astype(jnp.float32),
        lax.psum_scatter(
            out_bias_share.astype(jnp.bfloat16), "dp", scatter_dimension=0, tiled=True
        ).astype(jnp.float32),
    )
    return (
        jnp.stack(outputs),
        jnp.stack(token_grads),
        grad_cond,
        shares[0],
        shares[1],
        shares[2],
        shares[3],
        shares[4],
        shares[5],
        shares[6],
        shares[7],
        shares[8],
        shares[9],
    )


def solution(mesh):
    in_specs = (
        P(None, ("dp", "tensor"), None),
        P(None, "dp", None),
        P(None, ("dp", "tensor"), None),
        P(None, "dp", "tensor"),
        P(None, ("tensor", "dp")),
        P("dp", "tensor", None),
        P("tensor", "dp"),
        P("tensor", None, "dp"),
        P(("tensor", "dp")),
        P("dp", "tensor"),
        P(("tensor", "dp")),
        P("tensor", "dp"),
        P(("tensor", "dp")),
    )
    out_specs = (
        P(None, ("dp", "tensor"), None),
        P(None, ("dp", "tensor"), None),
        P(None, "dp", None),
        P(None, "dp", "tensor"),
        P(None, ("tensor", "dp")),
        P("dp", "tensor", None),
        P("tensor", "dp"),
        P("tensor", None, "dp"),
        P(("tensor", "dp")),
        P("dp", "tensor"),
        P(("tensor", "dp")),
        P("tensor", "dp"),
        P(("tensor", "dp")),
    )
    return jax.shard_map(body, mesh=mesh, in_specs=in_specs, out_specs=out_specs, check_vma=False)
```
